32 devices in a mesh: dp: 4 (over x, core), context: 4 (over z), tensor: 2 (over y).
Axes of the slice: x: 2, y: 2, z: 4, core: 2. Of those that a mesh axis runs over, the one named last changes fastest.
Arguments:
- normed: bfloat16 [4, 1536, 8192], P('dp', 'context', 'tensor'), may hold values from -8 to 8
- frozen_query_base: bfloat16 [4, 1536, 8192], P('dp', 'context', 'tensor'), may hold values from -66 to 66
- frozen_key_base: bfloat16 [4, 1536, 1024], P('dp', 'context', 'tensor'), may hold values from -3 to 3
- frozen_value_base: bfloat16 [4, 1536, 1024], P('dp', 'context', 'tensor'), may hold values from -4 to 4
- adapter_down_weight: bfloat16 [8192, 48], P('tensor'), may hold values from -0.0625 to 0.0625
- query_up_weight: bfloat16 [16, 8192], P(None, 'tensor'), may hold values from -0.29882812 to 0.29882812
- key_value_up_weight: bfloat16 [2, 16, 1024], P(None, None, 'tensor'), may hold values from -0.29882812 to 0.29882812
- output_gradient: bfloat16 [4, 1536, 8192], P('dp', 'context', 'tensor'), may hold values from -0.078125 to 0.078125
Outputs:
- attended: bfloat16 [4, 1536, 8192], P('dp', 'context', 'tensor')
- grad_a: float32 [8192, 48], P('tensor')
- query_up_gradient: float32 [16, 8192], P(None, 'tensor')
- grad_bkv: float32 [2, 16, 1024], P(None, None, 'tensor')
The draws below stay inside these ranges and needn't reach their ends.
All inputs are finite; a program needn't handle non-finite values.
Results may differ from the reference program's by a relative error of at most 0.012.
Values may be sent and summed in bfloat16 or wider, within the bound.
No kernel may reach another device: no remote copies, remote signals or barrier semaphores. Data moves between devices by JAX's collectives and lax.ppermute only.
A program may use at most 128 MiB of HBM per device.

```python
import jax
import jax.numpy as jnp
from jax import lax

MODEL_WIDTH = 8192
QUERY_HEAD_COUNT = 64
KEY_VALUE_HEADS = 8
HEAD_SIZE = 128
ADAPTER_DEPTH = 16
TOK_DEV = 384
LENGTH = 1536
SEQS = 4


def drawn(key):
    key_x = jax.random.fold_in(key, 101)
    key_k = jax.random.fold_in(key, 102)
    key_q = jax.random.fold_in(key, 103)
    hidden_x = jnp.clip(jax.random.normal(key_x, (SEQS, LENGTH, MODEL_WIDTH), jnp.float32), -4.0, 4.0)
    key_vals = jnp.clip(jax.random.normal(key_k, (SEQS, LENGTH, KEY_VALUE_HEADS, HEAD_SIZE), jnp.float32), -3.0, 3.0)
    query_vals = jnp.clip(jax.random.normal(key_q, (SEQS, LENGTH, QUERY_HEAD_COUNT, HEAD_SIZE), jnp.float32), -3.0, 3.0)
    return (hidden_x, query_vals.reshape(SEQS, LENGTH, QUERY_HEAD_COUNT * HEAD_SIZE), key_vals.reshape(SEQS, LENGTH, KEY_VALUE_HEADS * HEAD_SIZE))


def draw_normed(key, part):
    return drawn(key)[0].astype(jnp.bfloat16)


def draw_frozen_query_base(key, part):
    return drawn(key)[1].astype(jnp.bfloat16)


def draw_frozen_key_base(key, part):
    return drawn(key)[2].astype(jnp.bfloat16)


def levels(key, dims, cuts, smallest, high):
    level = 1.0
    for position, blocks in cuts:
        steps = jax.random.uniform(jax.random.fold_in(jax.random.fold_in(key, 6), position), (blocks,), jnp.float32, smallest / len(cuts), high / len(cuts))
        level = level * jnp.repeat(jnp.exp(steps), dims[position] // blocks).reshape((-1,) + (1,) * (len(dims) - 1 - position))
    return level


def noise(own_key, extent, spread, reach, split=(), dtype=jnp.bfloat16):
    drawn = jax.random.normal(own_key, extent, jnp.float32) * spread
    if len(split) > 0:
        drawn = levels(own_key, extent, split, -0.22, 0.18) * drawn
    return jnp.clip(drawn, min=-reach, max=reach).astype(dtype)


def setup_inputs(seed: int = 0) -> dict:
    arg_keys = jax.random.split(jax.random.key(seed), 9)
    normed = draw_normed(jax.random.fold_in(arg_keys[8], 71), 0)
    frozen_query_base = draw_frozen_query_base(jax.random.fold_in(arg_keys[8], 71), 0)
    frozen_key_base = draw_frozen_key_base(jax.random.fold_in(arg_keys[8], 71), 0)
    frozen_value_base = noise(arg_keys[3], (SEQS, LENGTH, KEY_VALUE_HEADS * HEAD_SIZE), 1.0, 4.0, ((0, 4), (1, 4), (2, 2)))
    adapter_down_weight = noise(arg_keys[4], (MODEL_WIDTH, 3 * ADAPTER_DEPTH), MODEL_WIDTH ** -0.5, 0.0625, ((0, 2),))
    query_up_weight = noise(arg_keys[5], (ADAPTER_DEPTH, QUERY_HEAD_COUNT * HEAD_SIZE), 0.05, 0.29882812, ((1, 2),))
    key_value_up_weight = noise(arg_keys[6], (2, ADAPTER_DEPTH, KEY_VALUE_HEADS * HEAD_SIZE), 0.05, 0.29882812, ((2, 2),))
    output_gradient = noise(arg_keys[7], (SEQS, LENGTH, QUERY_HEAD_COUNT * HEAD_SIZE), (SEQS * LENGTH) ** -0.5, 0.078125, ((0, 4), (1, 4), (2, 2)))
    return {"normed": normed, "frozen_query_base": frozen_query_base, "frozen_key_base": frozen_key_base, "frozen_value_base": frozen_value_base, "adapter_down_weight": adapter_down_weight, "query_up_weight": query_up_weight, "key_value_up_weight": key_value_up_weight, "output_gradient": output_gradient}


adapter_scale = 2.0


def attend(query_rows, key_heads, value_heads, grads, allowed):
    scale = HEAD_SIZE ** -0.5
    high = lax.Precision.HIGHEST
    query_full = query_rows.astype(jnp.float32)
    key_full = key_heads.astype(jnp.float32)
    value_full = value_heads.astype(jnp.float32)
    grad_full = grads.astype(jnp.float32)
    scores = jnp.einsum("tgrd,ugd->grtu", query_full, key_full, precision=high) * scale
    masked = jnp.where(allowed, scores, -jnp.inf)
    highest = jnp.max(masked, axis=-1, keepdims=True)
    weights = jnp.exp(masked - highest)
    probs = weights / jnp.sum(weights, axis=-1, keepdims=True)
    probs_low = probs.astype(jnp.bfloat16).astype(jnp.float32)
    output = jnp.einsum("grtu,ugd->tgrd", probs_low, value_full, precision=high)
    prob_grad = jnp.einsum("tgrd,ugd->grtu", grad_full, value_full, precision=high)
    row_dot = jnp.sum(probs * prob_grad, axis=-1, keepdims=True)
    score_grad = (probs * (prob_grad - row_dot) * scale).astype(jnp.bfloat16).astype(jnp.float32)
    query_gradient = jnp.einsum("grtu,ugd->tgrd", score_grad, key_full, precision=high)
    key_gradient = jnp.einsum("grtu,tgrd->ugd", score_grad, query_full, precision=high)
    value_gradient = jnp.einsum("grtu,tgrd->ugd", probs_low, grad_full, precision=high)
    return output, query_gradient, key_gradient, value_gradient


def grouped(query_rows, key_heads, value_heads, grads):
    blocks = query_rows.shape[0] // TOK_DEV
    row_ids = lax.broadcasted_iota(jnp.int32, (TOK_DEV, TOK_DEV), 0)
    col_ids = lax.broadcasted_iota(jnp.int32, (TOK_DEV, TOK_DEV), 1)
    causal = col_ids <= row_ids

    def split_rows(array):
        return array.reshape((blocks, TOK_DEV) + array.shape[1:])

    def one_group(pieces):
        return attend(pieces[0], pieces[1], pieces[2], pieces[3], causal)

    results = lax.map(one_group, (split_rows(query_rows), split_rows(key_heads), split_rows(value_heads), split_rows(grads)))
    return tuple(item.reshape((blocks * TOK_DEV,) + item.shape[2:]) for item in results)


def reference(normed, frozen_query_base, frozen_key_base, frozen_value_base, adapter_down_weight, query_up_weight, key_value_up_weight, output_gradient):
    row_total = SEQS * LENGTH
    flattened = normed.reshape(row_total, MODEL_WIDTH)
    reduced_projection = jnp.dot(flattened, adapter_down_weight, preferred_element_type=jnp.float32).astype(jnp.bfloat16)
    query_rows = (frozen_query_base.reshape(row_total, QUERY_HEAD_COUNT * HEAD_SIZE).astype(jnp.float32) + adapter_scale * jnp.dot(reduced_projection[:, :ADAPTER_DEPTH], query_up_weight, preferred_element_type=jnp.float32)).astype(jnp.bfloat16)
    key_row_block = (frozen_key_base.reshape(row_total, KEY_VALUE_HEADS * HEAD_SIZE).astype(jnp.float32) + adapter_scale * jnp.dot(reduced_projection[:, ADAPTER_DEPTH:2 * ADAPTER_DEPTH], key_value_up_weight[0], preferred_element_type=jnp.float32)).astype(jnp.bfloat16)
    value_row_block = (frozen_value_base.reshape(row_total, KEY_VALUE_HEADS * HEAD_SIZE).astype(jnp.float32) + adapter_scale * jnp.dot(reduced_projection[:, 2 * ADAPTER_DEPTH:], key_value_up_weight[1], preferred_element_type=jnp.float32)).astype(jnp.bfloat16)
    per_group = QUERY_HEAD_COUNT // KEY_VALUE_HEADS
    half_heads = per_group // 2
    offset = TOK_DEV // 2
    query_heads = query_rows.reshape(SEQS, LENGTH, KEY_VALUE_HEADS, per_group, HEAD_SIZE)
    grad_heads = output_gradient.reshape(SEQS, LENGTH, KEY_VALUE_HEADS, per_group, HEAD_SIZE)
    key_heads = key_row_block.reshape(SEQS, LENGTH, KEY_VALUE_HEADS, HEAD_SIZE)
    value_heads = value_row_block.reshape(SEQS, LENGTH, KEY_VALUE_HEADS, HEAD_SIZE)

    def rolled(array):
        return jnp.roll(array, -offset, axis=0)

    def unrolled(array):
        return jnp.roll(array, offset, axis=0)

    outputs, query_grads, key_grads, value_grads = [], [], [], []
    for which in range(SEQS):
        straight = grouped(query_heads[which, :, :, :half_heads], key_heads[which], value_heads[which], grad_heads[which, :, :, :half_heads])
        moved = grouped(rolled(query_heads[which, :, :, half_heads:]), rolled(key_heads[which]), rolled(value_heads[which]), rolled(grad_heads[which, :, :, half_heads:]))
        outputs.append(jnp.concatenate([straight[0], unrolled(moved[0])], axis=2))
        query_grads.append(jnp.concatenate([straight[1], unrolled(moved[1])], axis=2))
        key_grads.append(straight[2] + unrolled(moved[2]))
        value_grads.append(straight[3] + unrolled(moved[3]))
    attended = jnp.stack(outputs).reshape(SEQS, LENGTH, QUERY_HEAD_COUNT * HEAD_SIZE).astype(jnp.bfloat16)
    query_gradient = jnp.stack(query_grads).reshape(row_total, QUERY_HEAD_COUNT * HEAD_SIZE).astype(jnp.bfloat16)
    key_gradient = jnp.stack(key_grads).reshape(row_total, KEY_VALUE_HEADS * HEAD_SIZE).astype(jnp.bfloat16)
    value_gradient = jnp.stack(value_grads).reshape(row_total, KEY_VALUE_HEADS * HEAD_SIZE).astype(jnp.bfloat16)
    spanning_axis = (((0,), (0,)), ((), ()))
    query_up_gradient = adapter_scale * lax.dot_general(reduced_projection[:, :ADAPTER_DEPTH], query_gradient, spanning_axis, preferred_element_type=jnp.float32)
    key_up_gradient = adapter_scale * lax.dot_general(reduced_projection[:, ADAPTER_DEPTH:2 * ADAPTER_DEPTH], key_gradient, spanning_axis, preferred_element_type=jnp.float32)
    value_up_gradient = adapter_scale * lax.dot_general(reduced_projection[:, 2 * ADAPTER_DEPTH:], value_gradient, spanning_axis, preferred_element_type=jnp.float32)
    inner_product = (((1,), (1,)), ((), ()))
    reduced_projection_gradient = (adapter_scale * jnp.concatenate([
        lax.dot_general(query_gradient, query_up_weight, inner_product, preferred_element_type=jnp.float32),
        lax.dot_general(key_gradient, key_value_up_weight[0], inner_product, preferred_element_type=jnp.float32),
        lax.dot_general(value_gradient, key_value_up_weight[1], inner_product, preferred_element_type=jnp.float32)], axis=1)).astype(jnp.bfloat16)
    grad_a = lax.dot_general(flattened, reduced_projection_gradient, spanning_axis, preferred_element_type=jnp.float32)
    return attended, grad_a, query_up_gradient, jnp.stack([key_up_gradient, value_up_gradient])
```

```python
import functools
import math

import jax
import jax.numpy as jnp
from jax import lax
from jax.experimental import pallas as pl
from jax.experimental.pallas import tpu as pltpu
from jax.sharding import PartitionSpec as P

QUERY_HEAD_COUNT = 64
KEY_VALUE_HEADS = 8
HEAD_SIZE = 128
HALF_HEADS = QUERY_HEAD_COUNT // KEY_VALUE_HEADS // 2
GROUP_WIDTH = HALF_HEADS * HEAD_SIZE
VMEM_LIMIT = 40 * 1024 * 1024
F32, BF16 = jnp.float32, jnp.bfloat16
adapter_scale = 2.0
score_scale = HEAD_SIZE ** (-0.5)


def dot_nn(a, b):
    return lax.dot_general(a, b, (((1,), (0,)), ((), ())), preferred_element_type=F32)


def dot_nt(a, b):
    return lax.dot_general(a, b, (((1,), (1,)), ((), ())), preferred_element_type=F32)


def params(**more):
    return pltpu.CompilerParams(vmem_limit_bytes=VMEM_LIMIT, **more)


def swapped(value, axis, bit):
    count = lax.axis_size(axis)
    return lax.ppermute(value, axis, [(source, source ^ bit) for source in range(count)])


def shifted(value, axis, steps):
    count = lax.axis_size(axis)
    return lax.ppermute(value, axis, [(source, (source + steps) % count) for source in range(count)])


def bits_of(axis):
    return [1 << k for k in range(int(math.log2(lax.axis_size(axis))))]


def low_rank_body(steps, normed, down, out, total):
    index = pl.program_id(0)
    part = dot_nt(normed[...], down[...])

    @pl.when(index == 0)
    def _():
        total[...] = part

    @pl.when(index > 0)
    def _():
        total[...] += part

    @pl.when(index == steps - 1)
    def _():
        out[...] = total[...].T


def low_rank_terms(normed, down):
    rows, width = normed.shape
    depth = down.shape[0]
    block = min(width, 1024)
    steps = width // block
    return pl.pallas_call(
        functools.partial(low_rank_body, steps),
        grid=(steps,),
        in_specs=[
            pl.BlockSpec((rows, block), lambda i: (0, i)),
            pl.BlockSpec((depth, block), lambda i: (0, i)),
        ],
        out_specs=pl.BlockSpec((depth, rows), lambda i: (0, 0)),
        out_shape=jax.ShapeDtypeStruct((depth, rows), F32),
        scratch_shapes=[pltpu.VMEM((rows, depth), F32)],
        compiler_params=params(),
    )(normed, down)


def project_body(mine, other, key_base, value_base, up, low, low_t, keys, values, send):
    depth = up.shape[1]
    rows, width = key_base.shape
    half = rows // 2
    total = mine[...] + other[...]
    rounded_t = total.astype(BF16)
    rounded = total.T.astype(BF16)
    low_t[...] = rounded_t
    low[...] = rounded
    for place, base, out in ((0, key_base, keys), (1, value_base, values)):
        term = dot_nn(rounded[:, (place + 1) * depth : (place + 2) * depth], up[place])
        whole = (base[...].astype(F32) + adapter_scale * term).astype(BF16)
        out[...] = whole
        send[:half, place * width : (place + 1) * width] = whole[half:]
    send[half:, :] = jnp.zeros((2 * depth, 2 * width), BF16)
    send[half:, :half] = rounded_t[depth:, half:]


def project(mine, other, key_base, value_base, up):
    rows, width = key_base.shape
    depth = up.shape[1]
    return pl.pallas_call(
        project_body,
        out_shape=[
            jax.ShapeDtypeStruct((rows, 3 * depth), BF16),
            jax.ShapeDtypeStruct((3 * depth, rows), BF16),
            jax.ShapeDtypeStruct((rows, width), BF16),
            jax.ShapeDtypeStruct((rows, width), BF16),
            jax.ShapeDtypeStruct((rows // 2 + 2 * depth, 2 * width), BF16),
        ],
        compiler_params=params(),
    )(mine, other, key_base, value_base, up)


def attend_block(keys, values, queries, grads):
    seen, half = keys.shape[0], queries.shape[0] // HALF_HEADS
    scores = dot_nt(keys, queries) * (score_scale * math.log2(math.e))
    prob_grad = dot_nt(values, grads)
    token = lax.rem(lax.broadcasted_iota(jnp.int32, (half, queries.shape[0]), 1), half)
    key = lax.broadcasted_iota(jnp.int32, (half, queries.shape[0]), 0)
    lower = jnp.where(key <= token, scores[seen - half :], -jnp.inf)
    if seen > half:
        lower = jnp.concatenate([scores[: seen - half], lower], axis=0)
    highest = jnp.max(lower, axis=0, keepdims=True)
    weights = jnp.exp2(lower - highest)
    probs = weights * (1.0 / jnp.sum(weights, axis=0, keepdims=True))
    probs_low = probs.astype(BF16)
    row_dot = jnp.sum(probs * prob_grad, axis=0, keepdims=True)
    score_grad = (probs * (prob_grad - row_dot)).astype(BF16)
    output = dot_nn(values.T, probs_low)
    value_grad = dot_nn(probs_low, grads)
    key_grad = dot_nn(score_grad, queries)
    query_grad = dot_nn(keys.T, score_grad)
    return output, query_grad, key_grad, value_grad


def attend_body(moved, query_base, grads, keys, values, earlier, low, low_t, query_up, key_up, value_up, attended, up_grads, key_up_grad, value_up_grad, rank_grads, rank_back):
    rows = query_base.shape[0]
    half = rows // 2
    depth = query_up.shape[0]

    @pl.when(pl.program_id(0) == 0)
    def _():
        rank_grads[...] = jnp.zeros_like(rank_grads)
        if moved:
            rank_back[...] = jnp.zeros_like(rank_back)

    term = dot_nn(low[:, :depth], query_up[...])
    queries = (query_base[...].astype(F32) + adapter_scale * term).astype(BF16)
    own_keys, own_values = keys[...], values[...]
    gradients = grads[...]
    results = []
    for place in range(2):
        own = slice(place * half, (place + 1) * half)
        stacked = [
            jnp.concatenate(
                [whole[own, head * HEAD_SIZE : (head + 1) * HEAD_SIZE] for head in range(HALF_HEADS)]
            )
            for whole in (queries, gradients)
        ]
        if not moved:
            seen_keys, seen_values = own_keys[: (place + 1) * half], own_values[: (place + 1) * half]
        elif place == 0:
            seen_keys = jnp.concatenate([earlier[0][...], own_keys[:half]])
            seen_values = jnp.concatenate([earlier[1][...], own_values[:half]])
        else:
            seen_keys, seen_values = own_keys[half:], own_values[half:]
        output, query_grad, key_grad, value_grad = attend_block(seen_keys, seen_values, *stacked)
        output = output.astype(BF16).T
        for head in range(HALF_HEADS):
            attended[own, head * HEAD_SIZE : (head + 1) * HEAD_SIZE] = output[
                head * half : (head + 1) * half
            ]
        results.append((query_grad.astype(BF16), key_grad, value_grad))
    (query_0, *first), (query_1, *second) = results
    for place, up, out in ((1, key_up, key_up_grad), (2, value_up, value_up_grad)):
        one, two = first[place - 1], second[place - 1]
        if moved:
            own = jnp.concatenate([one[half:], two])
            back = one[:half].astype(BF16)
        else:
            own = jnp.concatenate([one + two[:half], two[half:]])
        own = own.astype(BF16)
        mine = slice(place * depth, (place + 1) * depth)
        gradient = dot_nn(low_t[mine, :], own)
        rank_grads[mine, :] += dot_nt(up[...], own)
        if moved:
            theirs = slice((place - 1) * depth, place * depth)
            gradient += dot_nn(earlier[2][theirs, :half], back)
            rank_back[theirs, :] += dot_nt(up[...], back)
        out[...] = gradient
    total = jnp.zeros((depth, rows), F32)
    for head in range(HALF_HEADS):
        columns = slice(head * HEAD_SIZE, (head + 1) * HEAD_SIZE)
        lanes = slice(head * half, (head + 1) * half)
        query_grad = jnp.concatenate([query_0[:, lanes], query_1[:, lanes]], axis=1)
        total += dot_nn(query_up[:, columns], query_grad)
        up_grads[:, columns] = dot_nt(low_t[:depth, :], query_grad)
    rank_grads[:depth, :] += total


def attend(moved, query_base, grads, keys, values, received, low, low_t, query_up, key_value_up, attended):
    rows, width = query_base.shape
    half = rows // 2
    depth = query_up.shape[0]
    count = keys.shape[1] // HEAD_SIZE
    ours = lambda i: (0, 2 * i + int(moved))
    head = lambda i: (0, i)
    fixed = lambda i: (0, 0)
    specs = [
        pl.BlockSpec((rows, GROUP_WIDTH), ours),
        pl.BlockSpec((rows, GROUP_WIDTH), ours),
        pl.BlockSpec((rows, HEAD_SIZE), head),
        pl.BlockSpec((rows, HEAD_SIZE), head),
        pl.BlockSpec(low.shape, fixed),
        pl.BlockSpec(low_t.shape, fixed),
        pl.BlockSpec((depth, GROUP_WIDTH), ours),
        pl.BlockSpec((None, depth, HEAD_SIZE), lambda i: (0, 0, i)),
        pl.BlockSpec((None, depth, HEAD_SIZE), lambda i: (1, 0, i)),
    ]
    args = [query_base, grads, keys, values, low, low_t, query_up, key_value_up, key_value_up]
    shapes = [
        jax.ShapeDtypeStruct((rows, width), BF16),
        jax.ShapeDtypeStruct((depth, width // 2), F32),
        jax.ShapeDtypeStruct((depth, count * HEAD_SIZE), F32),
        jax.ShapeDtypeStruct((depth, count * HEAD_SIZE), F32),
        jax.ShapeDtypeStruct(low_t.shape, F32),
    ]
    out_specs = [
        pl.BlockSpec((rows, GROUP_WIDTH), ours),
        pl.BlockSpec((depth, GROUP_WIDTH), head),
        pl.BlockSpec((depth, HEAD_SIZE), head),
        pl.BlockSpec((depth, HEAD_SIZE), head),
        pl.BlockSpec(low_t.shape, fixed),
    ]
    aliases = {}
    if moved:
        specs += [
            pl.BlockSpec((half, HEAD_SIZE), lambda i: (0, i)),
            pl.BlockSpec((half, HEAD_SIZE), lambda i: (0, count + i)),
            pl.BlockSpec((2 * depth, received.shape[1]), lambda i: (half // (2 * depth), 0)),
            pl.BlockSpec(memory_space=pl.ANY),
        ]
        args += [received, received, received, attended]
        aliases = {len(args) - 1: 0}
        shapes.append(jax.ShapeDtypeStruct((2 * depth, half), F32))
        out_specs.append(pl.BlockSpec((2 * depth, half), fixed))

    def body(*refs):
        main, rest = refs[:9], refs[9:]
        if moved:
            earlier, outs = rest[:3], rest[4:]
        else:
            earlier, outs = None, rest + (None,)
        attend_body(moved, *main[:4], earlier, *main[4:], *outs)

    return pl.pallas_call(
        body,
        grid=(count,),
        in_specs=specs,
        out_specs=out_specs,
        out_shape=shapes,
        input_output_aliases=aliases,
        compiler_params=params(),
        cost_estimate=pl.CostEstimate(
            flops=count * 1400 * 10**6, bytes_accessed=6 * 10**6, transcendentals=0
        ),
    )(*args)


def terms_body(place, mine, other, normed, up_grads, kv_grads, out):
    depth3 = mine.shape[0]
    width = normed.shape[1]
    rank = (mine[...] + other[...]).astype(BF16)
    out[:depth3, :width] = dot_nn(rank, normed[...]).astype(BF16)
    out[depth3:, :width] = up_grads[...].astype(BF16)
    out[:, width:] = jnp.zeros((out.shape[0], out.shape[1] - width), BF16)
    out[: kv_grads.shape[0], width : width + kv_grads.shape[1]] = kv_grads[...].astype(BF16)


def gradient_terms(place, mine, other, normed, up_grads, kv_grads):
    rows, width = normed.shape
    parts = kv_grads.shape[0]
    part = width // parts
    stages = int(math.log2(parts))
    lines = mine.shape[0] + up_grads.shape[1]

    def block(i, place):
        mask = 0
        for stage in range(stages):
            mask += (1 - (i >> (stages - 1 - stage)) % 2) << stage
        return place[0] ^ mask

    return pl.pallas_call(
        terms_body,
        grid_spec=pltpu.PrefetchScalarGridSpec(
            num_scalar_prefetch=1,
            grid=(parts,),
            in_specs=[
                pl.BlockSpec(mine.shape, lambda i, place: (0, 0)),
                pl.BlockSpec(mine.shape, lambda i, place: (0, 0)),
                pl.BlockSpec((rows, part), lambda i, place: (0, block(i, place))),
                pl.BlockSpec((None,) + up_grads.shape[1:], lambda i, place: (block(i, place), 0, 0)),
                pl.BlockSpec((None,) + kv_grads.shape[1:], lambda i, place: (block(i, place), 0, 0)),
            ],
            out_specs=pl.BlockSpec((None, lines, part + HEAD_SIZE), lambda i, place: (i, 0, 0)),
        ),
        out_shape=jax.ShapeDtypeStruct((parts, lines, part + HEAD_SIZE), BF16),
        compiler_params=params(),
    )(place, mine, other, normed, up_grads, kv_grads)


def on_device(
    normed,
    frozen_query_base,
    frozen_key_base,
    frozen_value_base,
    adapter_down_weight,
    query_up_weight,
    key_value_up_weight,
    output_gradient,
):
    tokens = normed[0]
    rows, width = tokens.shape
    half = rows // 2
    depth = query_up_weight.shape[0]
    query_width = query_up_weight.shape[1]
    kv_width = key_value_up_weight.shape[2]

    mine = low_rank_terms(tokens, adapter_down_weight.T)
    for bit in bits_of("tensor")[:-1]:
        mine = mine + swapped(mine, "tensor", bit)
    other = swapped(mine, "tensor", bits_of("tensor")[-1])
    low, low_t, keys, values, send = project(
        mine, other, frozen_key_base[0], frozen_value_base[0], key_value_up_weight
    )
    received = shifted(send, "context", 1)
    common = (low, low_t, query_up_weight, key_value_up_weight)
    attended, up_0, key_0, value_0, rank_0 = attend(
        False, frozen_query_base[0], output_gradient[0], keys, values, None, *common, None
    )
    attended, up_1, key_1, value_1, rank_1, rank_back = attend(
        True, frozen_query_base[0], output_gradient[0], keys, values, received, *common, attended
    )
    returned = shifted(rank_back, "context", -1)
    factors = jnp.concatenate(
        [
            jnp.full((2 * depth, 1), adapter_scale * score_scale, F32),
            jnp.full((depth, 1), adapter_scale, F32),
        ]
    )
    rank = rank_0 + rank_1 + jnp.pad(returned, ((depth, 0), (half, 0)))
    rank = rank * factors
    for bit in bits_of("tensor")[:-1]:
        rank = rank + swapped(rank, "tensor", bit)
    rank_other = swapped(rank, "tensor", bits_of("tensor")[-1])

    parts = lax.axis_size("dp")
    groups = query_width // (2 * GROUP_WIDTH)
    up = jnp.stack(
        [up_0.reshape(depth, groups, GROUP_WIDTH), up_1.reshape(depth, groups, GROUP_WIDTH)], axis=2
    ).reshape(depth, query_width)
    up = up * (adapter_scale * score_scale)
    up_parts = up.reshape(depth, parts, query_width // parts).transpose(1, 0, 2)
    kv = jnp.concatenate(
        [(key_0 + key_1) * (adapter_scale * score_scale), (value_0 + value_1) * adapter_scale]
    )
    if kv_width // HEAD_SIZE % parts == 0:
        kv_parts = kv.reshape(2 * depth, parts, kv_width // parts).transpose(1, 0, 2)
    else:
        kv_parts = kv.reshape(parts, 2 * depth // parts, kv_width)
    place = lax.axis_index("dp").reshape(1)
    held = gradient_terms(place, rank, rank_other, tokens, up_parts, kv_parts)
    for bit in bits_of("dp"):
        count = held.shape[0] // 2
        held = (held[count:].astype(F32) + swapped(held[:count], "dp", bit).astype(F32)).astype(BF16)
    held = held[0]
    for bit in bits_of("context"):
        held = (held.astype(F32) + swapped(held, "context", bit).astype(F32)).astype(BF16)
    pieces = {0: held}
    for bit in reversed(bits_of("dp")):
        for mask in list(pieces):
            pieces[mask ^ bit] = swapped(pieces[mask], "dp", bit)
    stacked = jnp.stack([pieces[mask] for mask in range(parts)])
    stacked = jnp.take(stacked, jnp.arange(parts) ^ place[0], axis=0)
    part = width // parts
    grad_a = stacked[:, : 3 * depth, :part].transpose(1, 0, 2).reshape(3 * depth, width).astype(F32)
    grad_up = stacked[:, 3 * depth :, :part].transpose(1, 0, 2).reshape(depth, width).astype(F32)
    grad_kv = stacked[:, : kv_parts.shape[1], part : part + kv_parts.shape[2]].astype(F32)
    if kv_parts.shape[1] == 2 * depth:
        grad_kv = grad_kv.transpose(1, 0, 2)
    return (attended[None], grad_a.T, grad_up, grad_kv.reshape(2, depth, kv_width))


def solution(mesh):
    in_specs = (
        P("dp", "context", "tensor"),
        P("dp", "context", "tensor"),
        P("dp", "context", "tensor"),
        P("dp", "context", "tensor"),
        P("tensor", None),
        P(None, "tensor"),
        P(None, None, "tensor"),
        P("dp", "context", "tensor"),
    )
    out_specs = (
        P("dp", "context", "tensor"),
        P("tensor", None),
        P(None, "tensor"),
        P(None, None, "tensor"),
    )
    return jax.shard_map(
        on_device, mesh=mesh, in_specs=in_specs, out_specs=out_specs, check_vma=False
    )
```

```python
import functools
import math

import jax
import jax.numpy as jnp
from jax import lax
from jax.experimental import pallas as pl
from jax.experimental.pallas import tpu as pltpu
from jax.sharding import PartitionSpec as P

QUERY_HEAD_COUNT = 64
KEY_VALUE_HEADS = 8
HEAD_SIZE = 128
HALF_HEADS = QUERY_HEAD_COUNT // KEY_VALUE_HEADS // 2
GROUP_WIDTH = HALF_HEADS * HEAD_SIZE
MIB = 1024 * 1024
ATTEND_MIB = 44
VMEM_WHOLE = pl.BlockSpec(memory_space=pltpu.VMEM)
IN_HBM = pl.BlockSpec(memory_space=pltpu.HBM)
F32, BF16 = jnp.float32, jnp.bfloat16
adapter_scale = 2.0
score_scale = HEAD_SIZE ** (-0.5)


def dot_nn(a, b):
    return lax.dot_general(a, b, (((1,), (0,)), ((), ())), preferred_element_type=F32)


def dot_nt(a, b):
    return lax.dot_general(a, b, (((1,), (1,)), ((), ())), preferred_element_type=F32)


def dot_tn(a, b):
    return lax.dot_general(a, b, (((0,), (0,)), ((), ())), preferred_element_type=F32)


def in_hbm(value):
    return pltpu.with_memory_space_constraint(value, pltpu.HBM)


def params(mebibytes):
    return pltpu.CompilerParams(vmem_limit_bytes=mebibytes * MIB)


def swapped(value, axis, bit):
    count = lax.axis_size(axis)
    return lax.ppermute(value, axis, [(source, source ^ bit) for source in range(count)])


def shifted(value, axis, steps):
    count = lax.axis_size(axis)
    return lax.ppermute(value, axis, [(source, (source + steps) % count) for source in range(count)])


def crossed(value, axis, steps, other_axis, bit):
    count, other_count = lax.axis_size(axis), lax.axis_size(other_axis)
    pairs = []
    for one in range(count):
        for two in range(other_count):
            target = (one + steps) % count * other_count + (two ^ bit)
            pairs.append((one * other_count + two, target))
    return lax.ppermute(value, (axis, other_axis), pairs)


def bits_of(axis):
    return [1 << k for k in range(int(math.log2(lax.axis_size(axis))))]


def low_rank_body(normed, down, out, sent, buffer, down_buffer, sems):
    blocks, rows, block = buffer.shape
    copies = [pltpu.make_async_copy(down, down_buffer, sems.at[blocks])]
    for i in range(blocks):
        source = normed.at[:, pl.ds(i * block, block)]
        copies.append(pltpu.make_async_copy(source, buffer.at[i], sems.at[i]))
    for copy in copies:
        copy.start()
    copies[0].wait()
    total = jnp.zeros((rows, down.shape[0]), F32)
    for i in range(blocks):
        copies[i + 1].wait()
        total += dot_nt(buffer[i], down_buffer[:, i * block : (i + 1) * block])
    whole = total.T
    out[...] = whole
    sent[...] = whole.astype(sent.dtype)


def low_rank_terms(normed, down):
    rows, width = normed.shape
    depth = down.shape[0]
    block = min(width, 512)
    blocks = width // block
    return pl.pallas_call(
        low_rank_body,
        in_specs=[IN_HBM] * 2,
        out_specs=[VMEM_WHOLE] * 2,
        out_shape=[jax.ShapeDtypeStruct((depth, rows), kind) for kind in (F32, BF16)],
        scratch_shapes=[
            pltpu.VMEM((blocks, rows, block), BF16),
            pltpu.VMEM((depth, width), BF16),
            pltpu.SemaphoreType.DMA((blocks + 1,)),
        ],
        compiler_params=params(16),
    )(normed, down)


def project_body(mine, other, key_base, value_base, up, low, low_t, low_blocks, keys, values, send):
    depth = up.shape[1]
    rows, width = key_base.shape
    half = rows // 2
    total = mine[...] + other[...].astype(F32)
    rounded_t = total.astype(BF16)
    rounded = total.T.astype(BF16)
    doubled = (adapter_scale * rounded.astype(F32)).astype(BF16)
    low_t[...] = rounded_t
    low[...] = doubled
    column_head = lax.broadcasted_iota(jnp.int32, (half, HALF_HEADS * depth), 1) // depth
    for place in range(2):
        wide = jnp.concatenate([rounded[place * half : (place + 1) * half, :depth]] * HALF_HEADS, axis=1)
        for head in range(HALF_HEADS):
            low_blocks[place, head * half : (head + 1) * half, :] = jnp.where(
                column_head == head, wide, jnp.zeros_like(wide)
            )
    for place, base, out in ((0, key_base, keys), (1, value_base, values)):
        term = dot_nn(doubled[:, (place + 1) * depth : (place + 2) * depth], up[place])
        whole = (base[...].astype(F32) + term).astype(BF16)
        out[...] = whole
        send[:half, place * width : (place + 1) * width] = whole[half:]
    send[half:, :] = jnp.zeros((2 * depth, 2 * width), BF16)
    send[half:, :half] = rounded_t[depth:, half:]


def project(mine, other, key_base, value_base, up):
    rows, width = key_base.shape
    depth = up.shape[1]
    return pl.pallas_call(
        project_body,
        in_specs=[VMEM_WHOLE] * 5,
        out_specs=[VMEM_WHOLE] * 6,
        out_shape=[
            jax.ShapeDtypeStruct((rows, 3 * depth), BF16),
            jax.ShapeDtypeStruct((3 * depth, rows), BF16),
            jax.ShapeDtypeStruct((2, HALF_HEADS * rows // 2, HALF_HEADS * depth), BF16),
            jax.ShapeDtypeStruct((rows, width), BF16),
            jax.ShapeDtypeStruct((rows, width), BF16),
            jax.ShapeDtypeStruct((rows // 2 + 2 * depth, 2 * width), BF16),
        ],
        compiler_params=params(8),
    )(mine, other, key_base, value_base, up)


def softmax_parts(scores, prob_grad, half):
    seen, lanes = scores.shape
    token = lax.broadcasted_iota(jnp.int32, (1, lanes), 1)
    first = jnp.zeros_like(token)
    for head in range(1, HALF_HEADS):
        first += jnp.where(token >= head * half, half, 0)
    key = lax.broadcasted_iota(jnp.int32, (half, lanes), 0)
    scaled = scores * (score_scale * math.log2(math.e))
    masked = jnp.where(key <= token - first, scaled[seen - half :], -jnp.inf)
    if seen > half:
        masked = jnp.concatenate([scaled[: seen - half], masked], axis=0)
    highest = jnp.max(masked, axis=0, keepdims=True)
    weights = jnp.exp2(masked - highest)
    probs = weights * (1.0 / jnp.sum(weights, axis=0, keepdims=True))
    weighted = probs * prob_grad
    row_dot = jnp.sum(weighted, axis=0, keepdims=True)
    return probs.astype(BF16), (weighted - probs * row_dot).astype(BF16)


def attend_body(moved, count, *refs):
    (query_hbm, grads_hbm, keys, values, low, low_t, low_blocks, query_up, key_value_up), refs = refs[:9], refs[9:]
    if moved:
        (received, up_before, kv_before, rank_before, _), refs = refs[:5], refs[5:]
        (attended, up_grads, kv_grads, rank, sent, sent_back), refs = refs[:6], refs[6:]
    else:
        (attended, up_grads, kv_grads, rank), refs = refs[:4], refs[4:]
    query_buffer, grads_buffer, out_buffer, key_sums, value_sums, key_back, value_back, in_sems, out_sems = refs
    rows = keys.shape[0]
    half = rows // 2
    depth = query_up.shape[0]
    columns_of = lambda i: pl.ds((2 * i + int(moved)) * GROUP_WIDTH, GROUP_WIDTH)
    copies = []
    for i in range(count):
        for place, (source, target) in enumerate(((query_hbm, query_buffer), (grads_hbm, grads_buffer))):
            copy = pltpu.make_async_copy(source.at[:, columns_of(i)], target.at[i], in_sems.at[place, i])
            copy.start()
            copies.append(copy)
    rank_query = [jnp.zeros((HALF_HEADS * depth, HALF_HEADS * half), F32)] * 2
    writes = []
    for i in range(count):
        head_columns = slice(i * HEAD_SIZE, (i + 1) * HEAD_SIZE)
        up_columns = slice((2 * i + int(moved)) * GROUP_WIDTH, (2 * i + int(moved) + 1) * GROUP_WIDTH)
        up = query_up[:, up_columns]
        up_stack = jnp.concatenate(
            [up[:, head * HEAD_SIZE : (head + 1) * HEAD_SIZE] for head in range(HALF_HEADS)]
        )
        own_keys, own_values = keys[:, head_columns], values[:, head_columns]
        if moved:
            back_keys = received[:half, head_columns]
            back_values = received[:half, count * HEAD_SIZE + i * HEAD_SIZE : count * HEAD_SIZE + (i + 1) * HEAD_SIZE]
            seen_keys = [jnp.concatenate([back_keys, own_keys[:half]]), own_keys[half:]]
            seen_values = [jnp.concatenate([back_values, own_values[:half]]), own_values[half:]]
        else:
            seen_keys = [own_keys[:half], own_keys]
            seen_values = [own_values[:half], own_values]
        copies[2 * i].wait()
        copies[2 * i + 1].wait()
        queries = (query_buffer[i].astype(F32) + dot_nn(low[:, :depth], up)).astype(BF16)
        gradients = grads_buffer[i]
        scores, prob_grads, stacked = [], [], []
        for place in range(2):
            own = slice(place * half, (place + 1) * half)
            query_stack, grad_stack = [
                jnp.concatenate(
                    [whole[own, head * HEAD_SIZE : (head + 1) * HEAD_SIZE] for head in range(HALF_HEADS)]
                )
                for whole in (queries, gradients)
            ]
            scores.append(dot_nt(seen_keys[place], query_stack))
            prob_grads.append(dot_nt(seen_values[place], grad_stack))
            stacked.append((jnp.concatenate([query_stack, low_blocks[place]], axis=1), grad_stack))
        key_grads, value_grads = [], []
        for place in range(2):
            own = slice(place * half, (place + 1) * half)
            probs, score_grad = softmax_parts(scores[place], prob_grads[place], half)
            output = dot_nn(seen_values[place].T, probs).astype(BF16).T
            for head in range(HALF_HEADS):
                out_buffer[i, own, head * HEAD_SIZE : (head + 1) * HEAD_SIZE] = output[
                    head * half : (head + 1) * half
                ]
            value_grads.append(dot_nn(probs, stacked[place][1]))
            key_grads.append(dot_nn(score_grad, stacked[place][0]))
            key_rank = dot_nt(up_stack, seen_keys[place]).astype(BF16)
            rank_query[place] = rank_query[place] + dot_nn(key_rank, score_grad)
        write = pltpu.make_async_copy(out_buffer.at[i], attended.at[:, columns_of(i)], out_sems.at[i])
        write.start()
        writes.append(write)
        if moved:
            own_grads = [jnp.concatenate([one[half:], two]) for one, two in (key_grads, value_grads)]
            back = key_grads[0][:half].astype(BF16)
            key_back[i] = back[:, :HEAD_SIZE]
            value_back[i] = value_grads[0][:half].astype(BF16)
        else:
            own_grads = [
                jnp.concatenate([one + two[:half], two[half:]]) for one, two in (key_grads, value_grads)
            ]
        key_grad, value_grad = [whole.astype(BF16) for whole in own_grads]
        key_sums[i] = key_grad[:, :HEAD_SIZE]
        value_sums[i] = value_grad
        up_stacked = dot_tn(key_grad[:, HEAD_SIZE:], own_keys)
        if moved:
            up_stacked += dot_tn(back[:, HEAD_SIZE:], back_keys)
        up_stacked *= adapter_scale * score_scale
        target = up_columns.start if moved else i * GROUP_WIDTH
        for head in range(HALF_HEADS):
            span = slice(target + head * HEAD_SIZE, target + (head + 1) * HEAD_SIZE)
            up_grads[:, span] = up_stacked[head * depth : (head + 1) * depth]
        if moved:
            start = 2 * i * GROUP_WIDTH
            up_grads[:, start : start + GROUP_WIDTH] = up_before[:, i * GROUP_WIDTH : (i + 1) * GROUP_WIDTH]
    key_factor = adapter_scale * score_scale
    for place, factor, sums, back_sums in (
        (0, key_factor, key_sums, key_back),
        (1, adapter_scale, value_sums, value_back),
    ):
        mine = slice((place + 1) * depth, (place + 2) * depth)
        theirs = slice(place * depth, (place + 1) * depth)
        total = jnp.zeros((rows, depth), F32)
        total_back = jnp.zeros((half, depth), F32)
        for i in range(count):
            head_columns = slice(i * HEAD_SIZE, (i + 1) * HEAD_SIZE)
            up = key_value_up[place, :, head_columns]
            gradient = dot_nn(low_t[mine, :], sums[i])
            total += dot_nt(sums[i], up)
            if moved:
                gradient += dot_nn(received[half + place * depth : half + (place + 1) * depth, :half], back_sums[i])
                total_back += dot_nt(back_sums[i], up)
            gradient *= factor
            if moved:
                gradient += kv_before[place, :, head_columns]
            kv_grads[place, :, head_columns] = gradient
        rank[mine, :] = factor * total.T
        if moved:
            sent_back[theirs, :] = (factor * total_back.T).astype(BF16)
    for place in range(2):
        total = jnp.zeros((depth, half), F32)
        for head in range(HALF_HEADS):
            total += rank_query[place][head * depth : (head + 1) * depth, head * half : (head + 1) * half]
        rank[:depth, place * half : (place + 1) * half] = key_factor * total
    if moved:
        whole = rank[...] + rank_before[...]
        rank[...] = whole
        sent[...] = whole.astype(BF16)
    for write in writes:
        write.wait()


def attend(query_base, grads, keys, values, low, low_t, low_blocks, query_up, key_value_up, received, so_far):
    moved = received is not None
    rows, width = query_base.shape
    half = rows // 2
    depth = query_up.shape[0]
    count = keys.shape[1] // HEAD_SIZE
    args = [query_base, grads, keys, values, low, low_t, low_blocks, query_up, key_value_up]
    specs = [IN_HBM] * 2 + [VMEM_WHOLE] * 7
    shapes = [
        jax.ShapeDtypeStruct((rows, width), BF16),
        jax.ShapeDtypeStruct((depth, width if moved else width // 2), F32),
        jax.ShapeDtypeStruct((2, depth, count * HEAD_SIZE), F32),
        jax.ShapeDtypeStruct(low_t.shape, F32),
    ]
    aliases = {}
    if moved:
        attended, up_grads, kv_grads, rank = so_far
        args += [received, up_grads, kv_grads, rank, attended]
        specs += [VMEM_WHOLE] * 4 + [IN_HBM]
        aliases = {len(args) - 1: 0}
        shapes += [
            jax.ShapeDtypeStruct(low_t.shape, BF16),
            jax.ShapeDtypeStruct((2 * depth, half), BF16),
        ]
    return pl.pallas_call(
        functools.partial(attend_body, moved, count),
        in_specs=specs,
        out_specs=[IN_HBM] + [VMEM_WHOLE] * (len(shapes) - 1),
        out_shape=shapes,
        input_output_aliases=aliases,
        scratch_shapes=[
            pltpu.VMEM((count, rows, GROUP_WIDTH), BF16),
            pltpu.VMEM((count, rows, GROUP_WIDTH), BF16),
            pltpu.VMEM((count, rows, GROUP_WIDTH), BF16),
            pltpu.VMEM((count, rows, HEAD_SIZE), BF16),
            pltpu.VMEM((count, rows, HEAD_SIZE), BF16),
            pltpu.VMEM((count, half, HEAD_SIZE), BF16),
            pltpu.VMEM((count, half, HEAD_SIZE), BF16),
            pltpu.SemaphoreType.DMA((2, count)),
            pltpu.SemaphoreType.DMA((count,)),
        ],
        compiler_params=params(ATTEND_MIB),
        cost_estimate=pl.CostEstimate(
            flops=count * 1400 * 10**6, bytes_accessed=6 * 10**6, transcendentals=0
        ),
    )(*args)


def kv_part(shape, parts):
    count, depth, width = shape
    if width // HEAD_SIZE % parts == 0:
        return count * depth, width // parts
    return count * depth // parts, width


def terms_body(parts, place, mine, other, back, back_other, normed, up_grads, kv_grads, out):
    depth, width = up_grads.shape
    part = width // parts
    half = back.shape[1]
    stages = int(math.log2(parts))
    lines, columns = kv_part(kv_grads.shape, parts)
    rank = mine[...] + other[...].astype(F32)
    returned = back[...].astype(F32) + back_other[...].astype(F32)
    later = jnp.concatenate([rank[:depth, half:], rank[depth:, half:] + returned])
    rank = jnp.concatenate([rank[:, :half], later], axis=1).astype(BF16)
    for i in range(parts):
        mask = sum((1 - (i >> (stages - 1 - stage)) % 2) << stage for stage in range(stages))
        index = place[0] ^ mask
        span = pl.ds(pl.multiple_of(index * part, HEAD_SIZE), part)
        out[i, : 3 * depth, :part] = dot_nn(rank, normed[:, span]).astype(BF16)
        out[i, 3 * depth :, :part] = up_grads[:, span].astype(BF16)
        out[i, :, part:] = jnp.zeros((4 * depth, HEAD_SIZE), BF16)
        if lines == 2 * depth:
            head_span = pl.ds(pl.multiple_of(index * columns, HEAD_SIZE), columns)
            for kind in range(2):
                out[i, kind * depth : (kind + 1) * depth, part : part + columns] = kv_grads[
                    kind, :, head_span
                ].astype(BF16)
        else:
            each = depth // lines
            row = pl.multiple_of(lax.rem(index, each) * lines, lines)
            out[i, :lines, part : part + columns] = kv_grads[
                index // each, pl.ds(row, lines), :
            ].astype(BF16)


def gradient_terms(parts, place, mine, other, back, back_other, normed, up_grads, kv_grads):
    depth, width = up_grads.shape
    shape = (parts, 4 * depth, width // parts + HEAD_SIZE)
    return pl.pallas_call(
        functools.partial(terms_body, parts),
        in_specs=[pl.BlockSpec(memory_space=pltpu.SMEM)] + [VMEM_WHOLE] * 7,
        out_specs=VMEM_WHOLE,
        out_shape=jax.ShapeDtypeStruct(shape, BF16),
        compiler_params=params(16),
    )(place, mine, other, back, back_other, normed, up_grads, kv_grads)


def unpack_body(masks, depth, lines, columns, place, *refs):
    pieces, (down, up, kv) = refs[: len(masks)], refs[len(masks) :]
    part = down.shape[1] // len(masks)
    for mask, piece in zip(masks, pieces):
        index = place[0] ^ mask
        span = pl.ds(pl.multiple_of(index * part, HEAD_SIZE), part)
        down[:, span] = piece[: 3 * depth, :part].astype(F32)
        up[:, span] = piece[3 * depth :, :part].astype(F32)
        block = piece[:lines, part : part + columns].astype(F32)
        if lines == 2 * depth:
            kv[:, pl.ds(pl.multiple_of(index * columns, HEAD_SIZE), columns)] = block
        else:
            kv[pl.ds(pl.multiple_of(index * lines, lines), lines), :] = block


def unpack(place, pieces, depth, width, kv_width):
    masks = sorted(pieces)
    parts = len(masks)
    lines, columns = kv_part((2, depth, kv_width), parts)
    return pl.pallas_call(
        functools.partial(unpack_body, masks, depth, lines, columns),
        in_specs=[pl.BlockSpec(memory_space=pltpu.SMEM)] + [VMEM_WHOLE] * parts,
        out_specs=[VMEM_WHOLE] * 3,
        out_shape=[
            jax.ShapeDtypeStruct((3 * depth, width), F32),
            jax.ShapeDtypeStruct((depth, width), F32),
            jax.ShapeDtypeStruct((2 * depth, kv_width), F32),
        ],
        compiler_params=params(16),
    )(place, *[pieces[mask] for mask in masks])


def on_device(
    normed,
    frozen_query_base,
    frozen_key_base,
    frozen_value_base,
    adapter_down_weight,
    query_up_weight,
    key_value_up_weight,
    output_gradient,
):
    tokens = normed[0]
    width = tokens.shape[1]
    depth = query_up_weight.shape[0]
    kv_width = key_value_up_weight.shape[2]

    place = lax.axis_index("dp").reshape(1)
    mine, sent = low_rank_terms(in_hbm(tokens), in_hbm(adapter_down_weight.T))
    for bit in bits_of("tensor")[:-1]:
        mine = mine + swapped(mine, "tensor", bit)
        sent = mine.astype(BF16)
    other = swapped(sent, "tensor", bits_of("tensor")[-1])
    low, low_t, low_blocks, keys, values, send = project(
        mine, other, frozen_key_base[0], frozen_value_base[0], key_value_up_weight
    )
    received = shifted(send, "context", 1)
    common = (
        in_hbm(frozen_query_base[0]),
        in_hbm(output_gradient[0]),
        keys,
        values,
        low,
        low_t,
        low_blocks,
        query_up_weight,
        key_value_up_weight,
    )
    so_far = attend(*common, None, None)
    attended, up_grads, kv_grads, rank, sent, sent_back = attend(*common, received, so_far)
    for bit in bits_of("tensor")[:-1]:
        rank = rank + swapped(rank, "tensor", bit)
        sent = rank.astype(BF16)
        sent_back = (sent_back.astype(F32) + swapped(sent_back, "tensor", bit).astype(F32)).astype(BF16)
    last = bits_of("tensor")[-1]
    rank_other = swapped(sent, "tensor", last)
    back = shifted(sent_back, "context", -1)
    back_other = crossed(sent_back, "context", -1, "tensor", last)

    parts = lax.axis_size("dp")
    held = gradient_terms(
        parts, place, rank, rank_other, back, back_other, tokens, up_grads, kv_grads
    )
    for bit in bits_of("dp"):
        count = held.shape[0] // 2
        held = (held[count:].astype(F32) + swapped(held[:count], "dp", bit).astype(F32)).astype(BF16)
    held = held[0]
    for bit in bits_of("context"):
        held = (held.astype(F32) + swapped(held, "context", bit).astype(F32)).astype(BF16)
    pieces = {0: held}
    for bit in reversed(bits_of("dp")):
        for mask in list(pieces):
            pieces[mask ^ bit] = swapped(pieces[mask], "dp", bit)
    grad_a, grad_up, grad_kv = unpack(place, pieces, depth, width, kv_width)
    return (attended[None], grad_a.T, grad_up, grad_kv.reshape(2, depth, kv_width))


def solution(mesh):
    in_specs = (
        P("dp", "context", "tensor"),
        P("dp", "context", "tensor"),
        P("dp", "context", "tensor"),
        P("dp", "context", "tensor"),
        P("tensor", None),
        P(None, "tensor"),
        P(None, None, "tensor"),
        P("dp", "context", "tensor"),
    )
    out_specs = (
        P("dp", "context", "tensor"),
        P("tensor", None),
        P(None, "tensor"),
        P(None, None, "tensor"),
    )
    return jax.shard_map(
        on_device, mesh=mesh, in_specs=in_specs, out_specs=out_specs, check_vma=False
    )
```
